32 devices in a mesh: groups: 2 (over x), pool: 8 (over z, y), tensor: 2 (over core).
Axes of the slice: x: 2, y: 2, z: 4, core: 2. Of those that a mesh axis runs over, the one named last changes fastest.
Arguments:
- queries: bfloat16 [4096, 32, 128], P(('groups', 'pool'), 'tensor'), parts along dimension 0, may hold values from -8 to 8, as said below
- turn_cache: bfloat16 [4096, 2, 4, 128], P(('groups', 'pool'), None, 'tensor'), parts along dimension 0, may hold values from -6 to 6, as said below
- page_pool: bfloat16 [2560, 32, 2, 4, 128], P(('groups', 'pool'), None, None, 'tensor'), parts along dimension 0, may hold values from -6 to 6
- prefix_tokens: int32 [16], P('groups'), parts along dimension 0, may hold values from 2048 to 4096, as said below
- prefix_table: int32 [16, 128], P('groups'), parts along dimension 0, may hold values from 0 to 1279, as said below
- write_table: int32 [16, 8], P('groups'), parts along dimension 0, may hold values from 0 to 1279, as said below
- assignment: int32 [16], P('groups'), parts along dimension 0, may hold values from 0 to 7, each once
Outputs:
- attention: bfloat16 [4096, 32, 128], P(('groups', 'pool'), 'tensor'), parts along dimension 0
- updated_pool: bfloat16 [2560, 32, 2, 4, 128], P(('groups', 'pool'), None, None, 'tensor'), parts along dimension 0
The draws below stay inside these ranges and needn't reach their ends.
There are 2 independent parts, one for each index of `groups`. The reference program is written for one: setup_inputs(seed, part) draws one part's arguments, and reference() takes and returns one part's arrays. A program takes and returns all parts, laid end to end along the dimension named above; each array names one. Nothing has to cross between parts.
Inputs may be any that keep to these rules, and one draw needn't show every extreme that they name: `queries`: A float draw. `turn_cache`: A float draw. `prefix_tokens`: some conversation's prefix has exactly 4096 tokens. `prefix_table`: entry [c, j] is owner * 160 + slot, the page that holds prefix tokens j * 32 to (j + 1) * 32 - 1 of conversation c; entries past the prefix's last page are unused. Among one conversation's used pages at most 17 lie on one owner, and for every conversation exactly 17 lie on some owner. Slots are below 152. `write_table`: entry [c, j] is owner * 160 + slot; the pages of one conversation lie on different owners, all entries are distinct, and slots are 152 or more. `assignment`: each conversation is prefilled by one pool index.
All inputs are finite; a program needn't handle non-finite values.
Results may differ from the reference program's by a relative error of at most 0.004.
Values may be sent and summed in bfloat16 or wider, within the bound.
A program may use at most 128 MiB of HBM per device.

```python
import jax
import jax.numpy as jnp
from jax import lax

HD = 128
KVH = 4
QPK = 8
PAGE = 32
MAXP = 128
POOL_DEV = 160
NEW_DEV = 256
CAP = 17
N_POOL = 8


def draw_queries(key, part):
    key = jax.random.fold_in(key, 3)
    total_rows = N_POOL * NEW_DEV
    array_shape = (total_rows, KVH * QPK, HD)
    values = 2.5 * jax.random.truncated_normal(key, -3.2, 3.2, array_shape, jnp.float32)
    return values.astype(jnp.bfloat16)


def draw_turn_cache(key, part):
    key = jax.random.fold_in(key, 5)
    total_rows = N_POOL * NEW_DEV
    array_shape = (total_rows, 2, KVH, HD)
    values = jax.random.truncated_normal(key, -6.0, 6.0, array_shape, jnp.float32)
    return values.astype(jnp.bfloat16)


def draw_prefix_tokens(key, part):
    key = jax.random.fold_in(key, 7)
    length_key, longest_key = jax.random.split(key)
    full_length = MAXP * PAGE
    lengths = jax.random.randint(length_key, (N_POOL,), full_length // 2, full_length + 1)
    longest = jax.random.randint(longest_key, (), 0, N_POOL)
    lengths = jnp.where(jnp.arange(N_POOL) == longest, full_length, lengths)
    return lengths.astype(jnp.int32)


def table_row(subkey):
    crowd_key, order_key, slot_key = jax.random.split(subkey, 3)
    crowded = jax.random.randint(crowd_key, (), 0, N_POOL)
    ranking = jax.random.permutation(order_key, N_POOL * CAP)
    owners = jnp.arange(N_POOL * CAP) // CAP
    ranking = jnp.where(owners == crowded, ranking - N_POOL * CAP, ranking)
    ordering = jnp.argsort(ranking)
    owner_sequence = owners[ordering][:MAXP]
    slot_ids = jax.random.randint(slot_key, (MAXP,), 0, POOL_DEV - N_POOL)
    return owner_sequence * POOL_DEV + slot_ids


def draw_prefix_table(key, part):
    key = jax.random.fold_in(key, 11)
    subkeys = jax.random.split(key, N_POOL)
    return jax.vmap(table_row)(subkeys).astype(jnp.int32)


def draw_write_table(key, part):
    key = jax.random.fold_in(key, 13)
    owner_key, slot_key = jax.random.split(key)
    owners = jax.vmap(lambda subkey: jax.random.permutation(subkey, N_POOL)[:NEW_DEV // PAGE])(jax.random.split(owner_key, N_POOL))
    orders = jax.vmap(lambda subkey: jax.random.permutation(subkey, N_POOL))(jax.random.split(slot_key, N_POOL))
    conversation = jnp.arange(N_POOL)[:, None]
    slot_ids = POOL_DEV - N_POOL + orders[owners, conversation]
    return (owners * POOL_DEV + slot_ids).astype(jnp.int32)


def levels(key, shape, shards, low, top_value):
    level, own = 1.0, jax.random.fold_in(key, 6)
    for position, blocks in shards:
        draws = jnp.exp(jax.random.uniform(jax.random.fold_in(own, position), (blocks,), jnp.float32, low / len(shards), top_value / len(shards)))
        level = level * jnp.repeat(draws, shape[position] // blocks).reshape([-1 if axis == position else 1 for axis in range(len(shape))])
    return level


def bell_draw(own_key, dims, scale, limit, cuts=(), held_as=jnp.bfloat16):
    entries = scale * jax.random.normal(own_key, dims, jnp.float32)
    if cuts:
        entries = entries * levels(own_key, dims, cuts, -0.22, 0.18)
    return jnp.clip(entries, -limit, limit).astype(held_as)


def setup_inputs(seed: int = 0, part: int = 0) -> dict:
    arg_keys = jax.random.split(jax.random.key(seed), 8)
    part_splits = jax.random.split(jax.random.fold_in(arg_keys[7], part), 8)
    return {
        "queries": draw_queries(jax.random.fold_in(jax.random.fold_in(arg_keys[7], part), 71), part),
        "turn_cache": draw_turn_cache(jax.random.fold_in(jax.random.fold_in(arg_keys[7], part), 71), part),
        "page_pool": bell_draw(part_splits[2], (N_POOL * POOL_DEV, PAGE, 2, KVH, HD), 1.0, 6.0, ((0, 8), (3, 2))),
        "prefix_tokens": draw_prefix_tokens(jax.random.fold_in(jax.random.fold_in(arg_keys[7], part), 71), part),
        "prefix_table": draw_prefix_table(jax.random.fold_in(jax.random.fold_in(arg_keys[7], part), 71), part),
        "write_table": draw_write_table(jax.random.fold_in(jax.random.fold_in(arg_keys[7], part), 71), part),
        "assignment": jax.random.permutation(part_splits[6], N_POOL).astype(jnp.int32),
    }


def attend_device(device, queries, turn_cache, page_pool, prefix_tokens, prefix_table, assignment):
    conversation = assignment[device]
    grouped = lax.dynamic_slice_in_dim(queries, device * NEW_DEV, NEW_DEV, 0).astype(jnp.float32)
    grouped = grouped.reshape(NEW_DEV, KVH, QPK, HD)
    turn_rows = lax.dynamic_slice_in_dim(turn_cache, device * NEW_DEV, NEW_DEV, 0).astype(jnp.float32)
    gathered = page_pool[prefix_table[conversation]].astype(jnp.float32)
    gathered = gathered.reshape(MAXP * PAGE, 2, KVH, HD)
    all_keys = jnp.concatenate((gathered[:, 0], turn_rows[:, 0]), axis=0)
    all_values = jnp.concatenate((gathered[:, 1], turn_rows[:, 1]), axis=0)
    prefix_seen = jnp.arange(MAXP * PAGE, dtype=jnp.int32) < prefix_tokens[conversation]
    prefix_seen = jnp.broadcast_to(prefix_seen[None, :], (NEW_DEV, MAXP * PAGE))
    causal = jnp.arange(NEW_DEV)[None, :] <= jnp.arange(NEW_DEV)[:, None]
    allowed = jnp.concatenate((prefix_seen, causal), axis=1)
    scores = jnp.einsum("tgqd,sgd->gqts", grouped, all_keys) * (HD ** -0.5)
    scores = jnp.where(allowed[None, None], scores, -jnp.inf)
    row_max = jnp.max(scores, axis=-1, keepdims=True)
    weights = jnp.exp(scores - row_max)
    totals = jnp.sum(weights, axis=-1)
    rounded = lax.optimization_barrier(weights.astype(jnp.bfloat16)).astype(jnp.float32)
    mixed = jnp.einsum("gqts,sgd->gqtd", rounded, all_values) / totals[..., None]
    mixed = jnp.transpose(mixed, (2, 0, 1, 3)).reshape(NEW_DEV, KVH * QPK, HD)
    return mixed.astype(jnp.bfloat16)


def reference(queries, turn_cache, page_pool, prefix_tokens, prefix_table, write_table, assignment):
    devices = jnp.arange(N_POOL, dtype=jnp.int32)
    outputs = lax.map(lambda device: attend_device(device, queries, turn_cache, page_pool, prefix_tokens, prefix_table, assignment), devices)
    attention = outputs.reshape(N_POOL * NEW_DEV, KVH * QPK, HD)
    write_ids = write_table[assignment].reshape(-1)
    fresh_pages = turn_cache.reshape(N_POOL * (NEW_DEV // PAGE), PAGE, 2, KVH, HD)
    updated_pool = page_pool.at[write_ids].set(fresh_pages)
    return (attention, updated_pool)
```

```python
import functools

import jax
import jax.numpy as jnp
from jax import lax
from jax.experimental import pallas as pl
from jax.experimental.pallas import tpu as pltpu
from jax.sharding import PartitionSpec as P

LOG2E = 1.4426950408889634
HIDDEN = -1e30


def partner_pair(me, step, n):
    if n & (n - 1) == 0:
        other = 0
        bit = 1
        while bit < n:
            other = other + ((me // bit + step // bit) % 2) * bit
            bit *= 2
        return other, other
    return (me + step) % n, (me + n - step) % n


def kernel(
    n, cap, page_rows, row_block, slots_ref, seen_ref, fresh_pick_ref, q_ref, turn_ref, pool_ref,
    out_ref, written_ref,
    stage, recv, fresh_stage, fresh_recv, q_scr, wide, split, bias, m_scr, l_scr, acc,
    send_sem, recv_sem, fresh_send_sem, fresh_recv_sem,
):
    me = lax.axis_index("pool")
    new_len = q_ref.shape[0]
    head_dim = q_ref.shape[2]
    total_rows = q_scr.shape[1]
    page = page_rows // 4
    block_tokens = cap * page
    factor = head_dim ** (-0.5) * LOG2E

    barrier = pltpu.get_barrier_semaphore()

    @pl.loop(1, n)
    def _(step):
        to, source = partner_pair(me, step, n)
        pl.semaphore_signal(barrier, inc=1, device_id={"pool": to}, device_id_type=pl.DeviceIdType.MESH)

    def block_copy(step):
        to, source = partner_pair(me, step, n)
        return pltpu.make_async_remote_copy(
            src_ref=stage.at[step], dst_ref=recv.at[step],
            send_sem=send_sem.at[step], recv_sem=recv_sem.at[step],
            device_id={"pool": to}, device_id_type=pl.DeviceIdType.MESH,
        )

    def fresh_copy(step):
        to, source = partner_pair(me, step, n)
        return pltpu.make_async_remote_copy(
            src_ref=fresh_stage.at[step], dst_ref=fresh_recv.at[step],
            send_sem=fresh_send_sem.at[step], recv_sem=fresh_recv_sem.at[step],
            device_id={"pool": to}, device_id_type=pl.DeviceIdType.MESH,
        )

    def fill(step):
        to, source = partner_pair(me, step, n)
        for rank in range(cap):
            stage[step, pl.ds(rank * page_rows, page_rows), :] = pool_ref[slots_ref[to, rank]]

    fill(n - 1)
    pl.semaphore_wait(barrier, n - 1)
    block_copy(n - 1).start()

    @pl.loop(1, n - 1)
    def _(index):
        step = n - 1 - index
        fill(step)
        block_copy(step).start()

    @pl.loop(1, n)
    def _(step):
        to, source = partner_pair(me, step, n)
        fresh_stage[step] = turn_ref[fresh_pick_ref[to]]
        fresh_copy(step).start()

    written_ref[me] = turn_ref[fresh_pick_ref[me]]
    fill(0)

    for h in range(2):
        picked = q_ref[...].astype(jnp.float32)[:, h * 8:(h + 1) * 8, :]
        q_scr[h] = picked.reshape(total_rows, head_dim).astype(jnp.bfloat16)

    def separate(rows, tokens):
        wide[0:tokens * 4, :] = rows.astype(jnp.float32)
        for part in range(4):
            split[part, 0:tokens, :] = wide[pl.ds(part, tokens, stride=4), :].astype(jnp.bfloat16)

    def scores_of(h, start, tokens):
        return lax.dot_general(
            split[h, 0:tokens, :], q_scr[h, pl.ds(start, row_block), :],
            (((1,), (1,)), ((), ())), preferred_element_type=jnp.float32,
        )

    def weigh(h, weights, tokens):
        return lax.dot_general(
            split[2 + h, 0:tokens, :], weights.astype(jnp.bfloat16),
            (((0,), (0,)), ((), ())), preferred_element_type=jnp.float32,
        )

    separate(turn_ref[...].reshape(new_len * 4, head_dim), new_len)

    @pl.loop(0, total_rows // row_block)
    def _(index):
        start = pl.multiple_of(index * row_block, row_block)
        key = lax.broadcasted_iota(jnp.int32, (new_len, row_block), 0)
        query = lax.broadcasted_iota(jnp.int32, (new_len, row_block), 1) + start
        for h in range(2):
            s = jnp.where(key * 8 <= query, scores_of(h, start, new_len), HIDDEN)
            top = jnp.max(s, axis=0, keepdims=True)
            weights = jnp.exp2((s - top) * factor)
            m_scr[h, :, pl.ds(start, row_block)] = top
            l_scr[h, :, pl.ds(start, row_block)] = jnp.sum(weights, axis=0, keepdims=True)
            acc[h, :, pl.ds(start, row_block)] = weigh(h, weights, new_len)

    def attend(block_ref, source):
        token = lax.broadcasted_iota(jnp.int32, (page, 128), 0)
        for rank in range(cap):
            bias[pl.ds(rank * page, page), :] = jnp.where(token < seen_ref[source, rank], 0.0, HIDDEN)
        separate(block_ref[...], block_tokens)

        @pl.loop(0, total_rows // row_block)
        def _(index):
            start = pl.multiple_of(index * row_block, row_block)
            columns = pl.ds(start, row_block)
            hide = jnp.concatenate([bias[...]] * (row_block // 128), axis=1)
            for h in range(2):
                s = scores_of(h, start, block_tokens) + hide
                before = m_scr[h, :, columns]
                top = jnp.maximum(before, jnp.max(s, axis=0, keepdims=True))
                shrink = jnp.exp2((before - top) * factor)
                weights = jnp.exp2((s - top) * factor)
                m_scr[h, :, columns] = top
                l_scr[h, :, columns] = l_scr[h, :, columns] * shrink + jnp.sum(weights, axis=0, keepdims=True)
                acc[h, :, columns] = acc[h, :, columns] * shrink + weigh(h, weights, block_tokens)

    attend(stage.at[0], me)

    @pl.loop(1, n)
    def _(step):
        to, source = partner_pair(me, step, n)
        block_copy(step).wait_recv()
        attend(recv.at[step], source)

    @pl.loop(1, n)
    def _(step):
        to, source = partner_pair(me, step, n)
        fresh_copy(step).wait_recv()
        written_ref[source] = fresh_recv[step]

    out_block = row_block // 8

    @pl.loop(0, total_rows // row_block)
    def _(index):
        start = pl.multiple_of(index * row_block, row_block)
        columns = pl.ds(start, row_block)
        halves = []
        for h in range(2):
            mixed = acc[h, :, columns] / l_scr[h, :, columns]
            halves.append(mixed.T.reshape(out_block, 8, head_dim))
        out_ref[pl.ds(index * out_block, out_block)] = jnp.concatenate(halves, axis=1).astype(jnp.bfloat16)

    @pl.loop(1, n)
    def _(step):
        block_copy(step).wait_send()
        fresh_copy(step).wait_send()


def shards(queries, turn_cache, page_pool, prefix_tokens, prefix_table, write_table, assignment):
    n = lax.axis_size("pool")
    device = lax.axis_index("pool")
    pool_dev, page_size = page_pool.shape[0], page_pool.shape[1]
    head_dim = page_pool.shape[4]
    new_len = queries.shape[0]
    max_pages = prefix_table.shape[1]
    cap = (max_pages + n - 1) // n + 1
    page_rows = page_size * 4
    page_index = jnp.arange(max_pages)
    peer_index = jnp.arange(n)

    ordered = prefix_table[assignment]
    lengths = prefix_tokens[assignment]
    own_row = ordered[device]
    own_length = lengths[device]
    used = page_index[None, :] * page_size < lengths[:, None]
    requested = (ordered // pool_dev == device) & used
    from_peer = (own_row[None, :] // pool_dev == peer_index[:, None]) & (page_index[None, :] * page_size < own_length)
    marked = jnp.concatenate([requested, from_peer], axis=0)
    seen_count = jnp.minimum(own_length - page_index * page_size, page_size)
    values = jnp.concatenate([ordered % pool_dev, jnp.broadcast_to(seen_count[None, :], (n, max_pages))], axis=0)
    earlier = page_index[:, None] < page_index[None, :]
    rank = jnp.sum((marked[:, :, None] & earlier[None]).astype(jnp.int32), axis=1)
    pick = marked[:, None, :] & (rank[:, None, :] == jnp.arange(cap)[None, :, None])
    picked = jnp.sum(jnp.where(pick, values[:, None, :], 0), axis=2)
    slots, seen = picked[:n], picked[n:]

    incoming_write = write_table[assignment]
    own_write = incoming_write[device]
    write_hit = (own_write // pool_dev)[None, :] == peer_index[:, None]
    fresh_pick = jnp.sum(jnp.where(write_hit, jnp.arange(own_write.shape[0])[None, :], 0), axis=1)
    write_in = incoming_write // pool_dev == device
    target_slot = jnp.where(
        jnp.any(write_in, axis=1),
        jnp.sum(jnp.where(write_in, incoming_write % pool_dev, 0), axis=1),
        pool_dev,
    )

    total_rows = new_len * 8
    row_block = 512
    tokens = cap * page_size
    smem = pl.BlockSpec(memory_space=pltpu.SMEM)
    vmem = pl.BlockSpec(memory_space=pltpu.VMEM)
    bf16, f32 = jnp.bfloat16, jnp.float32
    attention, written = pl.pallas_call(
        functools.partial(kernel, n, cap, page_rows, row_block),
        out_shape=(
            jax.ShapeDtypeStruct(queries.shape, bf16),
            jax.ShapeDtypeStruct((n, page_rows, head_dim), bf16),
        ),
        in_specs=[smem, smem, smem, vmem, vmem, vmem],
        out_specs=(vmem, vmem),
        scratch_shapes=[
            pltpu.VMEM((n, cap * page_rows, head_dim), bf16),
            pltpu.VMEM((n, cap * page_rows, head_dim), bf16),
            pltpu.VMEM((n, page_rows, head_dim), bf16),
            pltpu.VMEM((n, page_rows, head_dim), bf16),
            pltpu.VMEM((2, total_rows, head_dim), bf16),
            pltpu.VMEM((max(tokens, new_len) * 4, head_dim), f32),
            pltpu.VMEM((4, max(tokens, new_len), head_dim), bf16),
            pltpu.VMEM((tokens, 128), f32),
            pltpu.VMEM((2, 1, total_rows), f32),
            pltpu.VMEM((2, 1, total_rows), f32),
            pltpu.VMEM((2, head_dim, total_rows), f32),
            pltpu.SemaphoreType.DMA((n,)),
            pltpu.SemaphoreType.DMA((n,)),
            pltpu.SemaphoreType.DMA((n,)),
            pltpu.SemaphoreType.DMA((n,)),
        ],
        compiler_params=pltpu.CompilerParams(
            collective_id=0, has_side_effects=True, vmem_limit_bytes=48 * 1024 * 1024
        ),
    )(
        slots, seen, fresh_pick, queries,
        turn_cache.reshape(new_len // page_size, page_rows, head_dim),
        page_pool.reshape(pool_dev, page_rows, head_dim),
    )
    updated_pool = page_pool.at[target_slot].set(
        written.reshape((n,) + page_pool.shape[1:]), mode="drop"
    )
    return (attention, updated_pool)


def solution(mesh):
    placed = (
        P(("groups", "pool"), "tensor", None),
        P(("groups", "pool"), None, "tensor", None),
        P(("groups", "pool"), None, None, "tensor", None),
        P("groups"),
        P("groups", None),
        P("groups", None),
        P("groups"),
    )
    return jax.shard_map(
        shards,
        mesh=mesh,
        in_specs=placed,
        out_specs=(
            P(("groups", "pool"), "tensor", None),
            P(("groups", "pool"), None, None, "tensor", None),
        ),
        check_vma=False,
    )
```

```python
import functools

import jax
import jax.numpy as jnp
from jax import lax
from jax.experimental import pallas as pl
from jax.experimental.pallas import tpu as pltpu
from jax.sharding import PartitionSpec as P

LOG2E = 1.4426950408889634
HIDDEN = -1e30


def partner_pair(me, step, n):
    if n & (n - 1) == 0:
        other = 0
        bit = 1
        while bit < n:
            other = other + ((me // bit + step // bit) % 2) * bit
            bit *= 2
        return other, other
    return (me + step) % n, (me + n - step) % n


def kernel(
    n, cap, wave, page_rows, row_block, plan_ref, q_hbm, turn_hbm, pool_hbm,
    out_ref, written_ref,
    q_ref, turn_ref, pool_ref, load_sem,
    stage, recv, rest_recv, fresh_stage, fresh_recv, q_scr, wide, split, bias, m_scr, l_scr, acc,
    send_sem, recv_sem, fresh_send_sem, fresh_recv_sem,
):
    me = lax.axis_index("pool")
    new_len = q_ref.shape[0]
    head_dim = q_ref.shape[2]
    total_rows = q_scr.shape[1]
    page = page_rows // 4
    full, rest = cap // wave, cap % wave
    factor = head_dim ** (-0.5) * LOG2E

    pool_load = pltpu.make_async_copy(pool_hbm, pool_ref, load_sem.at[0])
    turn_load = pltpu.make_async_copy(turn_hbm, turn_ref, load_sem.at[1])
    q_load = pltpu.make_async_copy(q_hbm, q_ref, load_sem.at[2])
    pool_load.start()
    turn_load.start()
    q_load.start()

    barrier = pltpu.get_barrier_semaphore()

    @pl.loop(1, n)
    def _(step):
        to, source = partner_pair(me, step, n)
        pl.semaphore_signal(barrier, inc=1, device_id={"pool": to}, device_id_type=pl.DeviceIdType.MESH)

    def remote(src, dst, send, receive, step):
        to, source = partner_pair(me, step, n)
        return pltpu.make_async_remote_copy(
            src_ref=src, dst_ref=dst, send_sem=send, recv_sem=receive,
            device_id={"pool": to}, device_id_type=pl.DeviceIdType.MESH,
        )

    def wave_copy(w, step):
        rows = pl.ds(pl.multiple_of(w * (wave * page_rows), page_rows), wave * page_rows)
        return remote(stage.at[step, rows], recv.at[w, step - 1], send_sem.at[w, step], recv_sem.at[w, step], step)

    def rest_copy(step):
        rows = pl.ds(full * wave * page_rows, rest * page_rows)
        return remote(stage.at[step, rows], rest_recv.at[step - 1], send_sem.at[full, step], recv_sem.at[full, step], step)

    def fresh_copy(step):
        return remote(fresh_stage.at[step], fresh_recv.at[step], fresh_send_sem.at[step], fresh_recv_sem.at[step], step)

    def fill(step, first, count):
        to, source = partner_pair(me, step, n)
        for r in range(count):
            rows = pl.ds(pl.multiple_of((first + r) * page_rows, page_rows), page_rows)
            stage[step, rows, :] = pool_ref[plan_ref[to, first + r]]

    pool_load.wait()

    @pl.loop(1, n)
    def _(step):
        fill(step, 0, wave)

    pl.semaphore_wait(barrier, n - 1)

    @pl.loop(1, n)
    def _(index):
        wave_copy(0, n - index).start()

    turn_load.wait()

    @pl.loop(1, n)
    def _(step):
        to, source = partner_pair(me, step, n)
        fresh_stage[step] = turn_ref[plan_ref[to, cap]]
        fresh_copy(step).start()

    @pl.loop(1, full)
    def _(w):
        @pl.loop(1, n)
        def _(index):
            fill(n - index, w * wave, wave)
            wave_copy(w, n - index).start()

    if rest:
        @pl.loop(1, n)
        def _(index):
            fill(n - index, full * wave, rest)
            rest_copy(n - index).start()

    written_ref[me] = turn_ref[plan_ref[me, cap]]
    fill(0, 0, cap)

    q_load.wait()
    for h in range(2):
        picked = q_ref[...].astype(jnp.float32)[:, h * 8:(h + 1) * 8, :]
        q_scr[h] = picked.reshape(total_rows, head_dim).astype(jnp.bfloat16)

    def separate(rows, tokens):
        wide[0:tokens * 4, :] = rows.reshape(tokens * 4, head_dim).astype(jnp.float32)
        for part in range(4):
            split[part, 0:tokens, :] = wide[pl.ds(part, tokens, stride=4), :].astype(jnp.bfloat16)

    def scores_of(h, start, tokens):
        return lax.dot_general(
            split[h, 0:tokens, :], q_scr[h, pl.ds(start, row_block), :],
            (((1,), (1,)), ((), ())), preferred_element_type=jnp.float32,
        )

    def weigh(h, weights, tokens):
        return lax.dot_general(
            split[2 + h, 0:tokens, :], weights.astype(jnp.bfloat16),
            (((0,), (0,)), ((), ())), preferred_element_type=jnp.float32,
        )

    separate(turn_ref[...], new_len)

    @pl.loop(0, total_rows // row_block)
    def _(index):
        start = pl.multiple_of(index * row_block, row_block)
        key = lax.broadcasted_iota(jnp.int32, (new_len, row_block), 0)
        query = lax.broadcasted_iota(jnp.int32, (new_len, row_block), 1) + start
        for h in range(2):
            s = jnp.where(key * 8 <= query, scores_of(h, start, new_len), HIDDEN)
            top = jnp.max(s, axis=0, keepdims=True)
            weights = jnp.exp2((s - top) * factor)
            m_scr[h, :, pl.ds(start, row_block)] = top
            l_scr[h, :, pl.ds(start, row_block)] = jnp.sum(weights, axis=0, keepdims=True)
            acc[h, :, pl.ds(start, row_block)] = weigh(h, weights, new_len)

    token = lax.broadcasted_iota(jnp.int32, (page, 128), 0)

    def hide(place, source, rank):
        at = place * page
        rows = pl.ds(at if isinstance(at, int) else pl.multiple_of(at, page), page)
        bias[rows, :] = jnp.where(token < plan_ref[n + source, rank], 0.0, HIDDEN)

    def hide_wave(first, count):
        @pl.loop(1, n)
        def _(step):
            to, source = partner_pair(me, step, n)
            for r in range(count):
                hide((step - 1) * count + r, source, first + r)

    def attend(rows, tokens):
        separate(rows, tokens)

        @pl.loop(0, total_rows // row_block)
        def _(index):
            start = pl.multiple_of(index * row_block, row_block)
            columns = pl.ds(start, row_block)
            hidden = jnp.concatenate([bias[0:tokens, :]] * (row_block // 128), axis=1)
            for h in range(2):
                s = scores_of(h, start, tokens) + hidden
                before = m_scr[h, :, columns]
                top = jnp.maximum(before, jnp.max(s, axis=0, keepdims=True))
                shrink = jnp.exp2((before - top) * factor)
                weights = jnp.exp2((s - top) * factor)
                m_scr[h, :, columns] = top
                l_scr[h, :, columns] = l_scr[h, :, columns] * shrink + jnp.sum(weights, axis=0, keepdims=True)
                acc[h, :, columns] = acc[h, :, columns] * shrink + weigh(h, weights, tokens)

    for rank in range(cap):
        hide(rank, me, rank)
    attend(stage[0], cap * page)

    @pl.loop(0, full)
    def _(w):
        hide_wave(w * wave, wave)

        @pl.loop(1, n)
        def _(step):
            wave_copy(w, step).wait_recv()

        attend(recv[w], (n - 1) * wave * page)

    @pl.loop(1, n)
    def _(step):
        to, source = partner_pair(me, step, n)
        fresh_copy(step).wait_recv()
        written_ref[source] = fresh_recv[step]

    if rest:
        hide_wave(full * wave, rest)

        @pl.loop(1, n)
        def _(step):
            rest_copy(step).wait_recv()

        attend(rest_recv[...], (n - 1) * rest * page)

    out_block = row_block // 8

    @pl.loop(0, total_rows // row_block)
    def _(index):
        start = pl.multiple_of(index * row_block, row_block)
        columns = pl.ds(start, row_block)
        halves = []
        for h in range(2):
            mixed = acc[h, :, columns] / l_scr[h, :, columns]
            halves.append(mixed.T.reshape(out_block, 8, head_dim))
        out_ref[pl.ds(index * out_block, out_block)] = jnp.concatenate(halves, axis=1).astype(jnp.bfloat16)

    @pl.loop(1, n)
    def _(step):
        @pl.loop(0, full)
        def _(w):
            wave_copy(w, step).wait_send()

        if rest:
            rest_copy(step).wait_send()
        fresh_copy(step).wait_send()


def plan_kernel(
    n, cap, pool_dev, page_size, assign_ref, tokens_ref, table_ref, write_ref,
    plan_ref, ordered, lengths, writes,
):
    me = lax.axis_index("pool")
    max_pages = table_ref.shape[1]
    for d in range(n):
        conversation = assign_ref[d]
        ordered[d:d + 1, :] = table_ref[pl.ds(conversation, 1), :]
        lengths[d:d + 1, :] = jnp.full((1, max_pages), tokens_ref[conversation], jnp.int32)
        writes[d:d + 1, :] = write_ref[pl.ds(conversation, 1), :]
    first = lax.broadcasted_iota(jnp.int32, (n, max_pages), 1) * page_size
    slot = ordered[...] - me * pool_dev
    requested = (slot >= 0) & (slot < pool_dev) & (first < lengths[...])
    row = jnp.broadcast_to(ordered[pl.ds(me, 1), :], (n, max_pages))
    length = jnp.broadcast_to(lengths[pl.ds(me, 1), :], (n, max_pages))
    place = row - lax.broadcasted_iota(jnp.int32, (n, max_pages), 0) * pool_dev
    landed = (place >= 0) & (place < pool_dev) & (first < length)
    values = jnp.concatenate([slot, jnp.minimum(length - first, page_size)], axis=0).astype(jnp.float32)
    marked = jnp.concatenate([jnp.where(requested, 1.0, 0.0), jnp.where(landed, 1.0, 0.0)], axis=0)
    earlier = (
        lax.broadcasted_iota(jnp.int32, (max_pages, max_pages), 0)
        < lax.broadcasted_iota(jnp.int32, (max_pages, max_pages), 1)
    )
    rank = jnp.dot(
        marked.astype(jnp.bfloat16), jnp.where(earlier, 1.0, 0.0).astype(jnp.bfloat16),
        preferred_element_type=jnp.float32,
    )
    rank = jnp.where(marked > 0.0, rank, -1.0)
    lane = lax.broadcasted_iota(jnp.int32, (2 * n, max_pages), 1)
    plan = jnp.zeros((2 * n, max_pages), jnp.float32)
    for r in range(cap):
        column = jnp.sum(jnp.where(rank == r, values, 0.0), axis=1, keepdims=True)
        plan = jnp.where(lane == r, column, plan)
    plan_ref[...] = plan.astype(jnp.int32)
    shape = writes.shape
    own = jnp.broadcast_to(writes[pl.ds(me, 1), :], shape)
    there = own - lax.broadcasted_iota(jnp.int32, shape, 0) * pool_dev
    page = lax.broadcasted_iota(jnp.int32, shape, 1).astype(jnp.float32)
    pick = jnp.sum(jnp.where((there >= 0) & (there < pool_dev), page, 0.0), axis=1, keepdims=True)
    here = writes[...] - me * pool_dev
    target = jnp.min(
        jnp.where((here >= 0) & (here < pool_dev), here, pool_dev).astype(jnp.float32), axis=1, keepdims=True
    )
    lane = lane[0:n, :]
    top = plan[0:n, :]
    top = jnp.where(lane == cap, pick, jnp.where(lane == cap + 1, target, top))
    plan_ref[0:n, :] = top.astype(jnp.int32)


def merge_kernel(
    n, cap, pool_dev, plan_ref, written_ref, attention_ref, pool_ref, out_ref, pool_out_ref,
    held, result, in_sem, out_sem, result_sem,
):
    chunks = in_sem.shape[0] - 1
    kept = pool_dev - n
    edges = [kept * chunk // chunks for chunk in range(chunks + 1)] + [pool_dev]
    spans = [pl.ds(low, high - low) for low, high in zip(edges[:-1], edges[1:])]
    loads = [pltpu.make_async_copy(pool_ref.at[span], held.at[span], in_sem.at[c]) for c, span in enumerate(spans)]
    stores = [pltpu.make_async_copy(held.at[span], pool_out_ref.at[span], out_sem.at[c]) for c, span in enumerate(spans)]
    result_in = pltpu.make_async_copy(attention_ref, result, result_sem.at[0])
    result_out = pltpu.make_async_copy(result, out_ref, result_sem.at[1])
    loads[-1].start()
    result_in.start()
    for load in loads[:-1]:
        load.start()
    loads[-1].wait()
    for d in range(n):
        @pl.when(plan_ref[d, cap + 1] < pool_dev)
        def _(d=d):
            held[plan_ref[d, cap + 1]] = written_ref[d]
    stores[-1].start()
    result_in.wait()
    result_out.start()
    for load, store in zip(loads[:-1], stores[:-1]):
        load.wait()
        store.start()
    for store in stores:
        store.wait()
    result_out.wait()


def shards(queries, turn_cache, page_pool, prefix_tokens, prefix_table, write_table, assignment):
    n = lax.axis_size("pool")
    pool_dev, page_size = page_pool.shape[0], page_pool.shape[1]
    head_dim = page_pool.shape[4]
    new_len = queries.shape[0]
    max_pages = prefix_table.shape[1]
    cap = (max_pages + n - 1) // n + 1
    page_rows = page_size * 4
    pages = page_pool.reshape(pool_dev, page_rows, head_dim)
    total_rows = new_len * 8
    row_block = 512
    wave = max(1, 24 // n)
    tokens = max(cap, (n - 1) * wave) * page_size
    smem = pl.BlockSpec(memory_space=pltpu.SMEM)
    vmem = pl.BlockSpec(memory_space=pltpu.VMEM)
    hbm = pl.BlockSpec(memory_space=pl.ANY)
    bf16, f32 = jnp.bfloat16, jnp.float32
    plan = pl.pallas_call(
        functools.partial(plan_kernel, n, cap, pool_dev, page_size),
        out_shape=jax.ShapeDtypeStruct((2 * n, max_pages), jnp.int32),
        in_specs=[smem, smem, vmem, vmem],
        out_specs=vmem,
        scratch_shapes=[
            pltpu.VMEM((n, max_pages), jnp.int32),
            pltpu.VMEM((n, max_pages), jnp.int32),
            pltpu.VMEM((n, write_table.shape[1]), jnp.int32),
        ],
    )(assignment, prefix_tokens, prefix_table, write_table)
    attention, written = pl.pallas_call(
        functools.partial(kernel, n, cap, wave, page_rows, row_block),
        out_shape=(
            jax.ShapeDtypeStruct(queries.shape, bf16),
            jax.ShapeDtypeStruct((n, page_rows, head_dim), bf16),
        ),
        in_specs=[smem, hbm, hbm, hbm],
        out_specs=(vmem, vmem),
        scratch_shapes=[
            pltpu.VMEM(queries.shape, bf16),
            pltpu.VMEM((new_len // page_size, page_rows, head_dim), bf16),
            pltpu.VMEM(pages.shape, bf16),
            pltpu.SemaphoreType.DMA((3,)),
            pltpu.VMEM((n, cap * page_rows, head_dim), bf16),
            pltpu.VMEM((cap // wave, n - 1, wave * page_rows, head_dim), bf16),
            pltpu.VMEM((n - 1, max(cap % wave, 1) * page_rows, head_dim), bf16),
            pltpu.VMEM((n, page_rows, head_dim), bf16),
            pltpu.VMEM((n, page_rows, head_dim), bf16),
            pltpu.VMEM((2, total_rows, head_dim), bf16),
            pltpu.VMEM((max(tokens, new_len) * 4, head_dim), f32),
            pltpu.VMEM((4, max(tokens, new_len), head_dim), bf16),
            pltpu.VMEM((tokens, 128), f32),
            pltpu.VMEM((2, 1, total_rows), f32),
            pltpu.VMEM((2, 1, total_rows), f32),
            pltpu.VMEM((2, head_dim, total_rows), f32),
            pltpu.SemaphoreType.DMA((cap // wave + 1, n)),
            pltpu.SemaphoreType.DMA((cap // wave + 1, n)),
            pltpu.SemaphoreType.DMA((n,)),
            pltpu.SemaphoreType.DMA((n,)),
        ],
        compiler_params=pltpu.CompilerParams(
            collective_id=0, has_side_effects=True, vmem_limit_bytes=56 * 1024 * 1024
        ),
    )(
        plan, queries,
        turn_cache.reshape(new_len // page_size, page_rows, head_dim),
        pages,
    )
    attention, updated_pool = pl.pallas_call(
        functools.partial(merge_kernel, n, cap, pool_dev),
        out_shape=(
            jax.ShapeDtypeStruct(queries.shape, bf16),
            jax.ShapeDtypeStruct(pages.shape, bf16),
        ),
        in_specs=[smem, vmem, hbm, hbm],
        out_specs=(hbm, hbm),
        scratch_shapes=[
            pltpu.VMEM(pages.shape, bf16),
            pltpu.VMEM(queries.shape, bf16),
            pltpu.SemaphoreType.DMA((9,)),
            pltpu.SemaphoreType.DMA((9,)),
            pltpu.SemaphoreType.DMA((2,)),
        ],
        compiler_params=pltpu.CompilerParams(vmem_limit_bytes=56 * 1024 * 1024),
    )(plan, written, attention, pages)
    updated_pool = updated_pool.reshape(page_pool.shape)
    return (attention, updated_pool)


def solution(mesh):
    placed = (
        P(("groups", "pool"), "tensor", None),
        P(("groups", "pool"), None, "tensor", None),
        P(("groups", "pool"), None, None, "tensor", None),
        P("groups"),
        P("groups", None),
        P("groups", None),
        P("groups"),
    )
    return jax.shard_map(
        shards,
        mesh=mesh,
        in_specs=placed,
        out_specs=(
            P(("groups", "pool"), "tensor", None),
            P(("groups", "pool"), None, None, "tensor", None),
        ),
        check_vma=False,
    )
```

```python
import functools

import jax
import jax.numpy as jnp
from jax import lax
from jax.experimental import pallas as pl
from jax.experimental.pallas import tpu as pltpu
from jax.sharding import PartitionSpec as P

LOG2E = 1.4426950408889634
HIDDEN = -1e30


def partner_pair(me, step, n):
    if n & (n - 1) == 0:
        other = 0
        bit = 1
        while bit < n:
            other = other + ((me // bit + step // bit) % 2) * bit
            bit *= 2
        return other, other
    return (me + step) % n, (me + n - step) % n


def kernel(
    n, cap, wave, page_rows, row_block, plan_ref, q_hbm, turn_hbm, pool_ref,
    out_ref, written_ref,
    q_ref, turn_ref, load_sem,
    stage, recv, rest_recv, fresh_stage, fresh_recv, q_scr, wide, split, bias, m_scr, l_scr, acc,
    send_sem, recv_sem, fresh_send_sem, fresh_recv_sem,
):
    me = lax.axis_index("pool")
    new_len = q_ref.shape[0]
    head_dim = q_ref.shape[2]
    total_rows = q_scr.shape[1]
    page = page_rows // 4
    full, rest = cap // wave, cap % wave
    factor = head_dim ** (-0.5) * LOG2E

    turn_load = pltpu.make_async_copy(turn_hbm, turn_ref, load_sem.at[0])
    q_load = pltpu.make_async_copy(q_hbm, q_ref, load_sem.at[1])
    turn_load.start()
    q_load.start()

    barrier = pltpu.get_barrier_semaphore()

    @pl.loop(1, n)
    def _(step):
        to, source = partner_pair(me, step, n)
        pl.semaphore_signal(barrier, inc=1, device_id={"pool": to}, device_id_type=pl.DeviceIdType.MESH)

    def remote(src, dst, send, receive, step):
        to, source = partner_pair(me, step, n)
        return pltpu.make_async_remote_copy(
            src_ref=src, dst_ref=dst, send_sem=send, recv_sem=receive,
            device_id={"pool": to}, device_id_type=pl.DeviceIdType.MESH,
        )

    def wave_copy(w, step):
        rows = pl.ds(pl.multiple_of(w * (wave * page_rows), page_rows), wave * page_rows)
        return remote(stage.at[step, rows], recv.at[w, step - 1], send_sem.at[w, step], recv_sem.at[w, step], step)

    def rest_copy(step):
        rows = pl.ds(full * wave * page_rows, rest * page_rows)
        return remote(stage.at[step, rows], rest_recv.at[step - 1], send_sem.at[full, step], recv_sem.at[full, step], step)

    def fresh_copy(step):
        return remote(fresh_stage.at[step], fresh_recv.at[step], fresh_send_sem.at[step], fresh_recv_sem.at[step], step)

    def fill(step, first, count):
        to, source = partner_pair(me, step, n)
        for r in range(count):
            rows = pl.ds(pl.multiple_of((first + r) * page_rows, page_rows), page_rows)
            stage[step, rows, :] = pool_ref[plan_ref[to, first + r]]

    @pl.loop(1, n)
    def _(step):
        fill(step, 0, wave)

    pl.semaphore_wait(barrier, n - 1)

    @pl.loop(1, n)
    def _(index):
        wave_copy(0, n - index).start()

    turn_load.wait()

    @pl.loop(1, n)
    def _(step):
        to, source = partner_pair(me, step, n)
        fresh_stage[step] = turn_ref[plan_ref[to, cap]]
        fresh_copy(step).start()

    @pl.loop(1, full)
    def _(w):
        @pl.loop(1, n)
        def _(index):
            fill(n - index, w * wave, wave)
            wave_copy(w, n - index).start()

    if rest:
        @pl.loop(1, n)
        def _(index):
            fill(n - index, full * wave, rest)
            rest_copy(n - index).start()

    written_ref[me] = turn_ref[plan_ref[me, cap]]
    fill(0, 0, cap)

    q_load.wait()
    for h in range(2):
        picked = q_ref[...].astype(jnp.float32)[:, h * 8:(h + 1) * 8, :]
        q_scr[h] = picked.reshape(total_rows, head_dim).astype(jnp.bfloat16)

    def separate(rows, tokens):
        wide[0:tokens * 4, :] = rows.reshape(tokens * 4, head_dim).astype(jnp.float32)
        for part in range(4):
            split[part, 0:tokens, :] = wide[pl.ds(part, tokens, stride=4), :].astype(jnp.bfloat16)

    def scores_of(h, start, tokens):
        return lax.dot_general(
            split[h, 0:tokens, :], q_scr[h, pl.ds(start, row_block), :],
            (((1,), (1,)), ((), ())), preferred_element_type=jnp.float32,
        )

    def weigh(h, weights, tokens):
        return lax.dot_general(
            split[2 + h, 0:tokens, :], weights.astype(jnp.bfloat16),
            (((0,), (0,)), ((), ())), preferred_element_type=jnp.float32,
        )

    separate(turn_ref[...], new_len)

    @pl.loop(0, total_rows // row_block)
    def _(index):
        start = pl.multiple_of(index * row_block, row_block)
        key = lax.broadcasted_iota(jnp.int32, (new_len, row_block), 0)
        query = lax.broadcasted_iota(jnp.int32, (new_len, row_block), 1) + start
        for h in range(2):
            s = jnp.where(key * 8 <= query, scores_of(h, start, new_len), HIDDEN)
            top = jnp.max(s, axis=0, keepdims=True)
            weights = jnp.exp2((s - top) * factor)
            m_scr[h, :, pl.ds(start, row_block)] = top
            l_scr[h, :, pl.ds(start, row_block)] = jnp.sum(weights, axis=0, keepdims=True)
            acc[h, :, pl.ds(start, row_block)] = weigh(h, weights, new_len)

    token = lax.broadcasted_iota(jnp.int32, (page, 128), 0)

    def hide(place, source, rank):
        at = place * page
        rows = pl.ds(at if isinstance(at, int) else pl.multiple_of(at, page), page)
        bias[rows, :] = jnp.where(token < plan_ref[n + source, rank], 0.0, HIDDEN)

    def hide_wave(first, count):
        @pl.loop(1, n)
        def _(step):
            to, source = partner_pair(me, step, n)
            for r in range(count):
                hide((step - 1) * count + r, source, first + r)

    def attend(rows, tokens):
        separate(rows, tokens)

        @pl.loop(0, total_rows // row_block)
        def _(index):
            start = pl.multiple_of(index * row_block, row_block)
            columns = pl.ds(start, row_block)
            hidden = jnp.concatenate([bias[0:tokens, :]] * (row_block // 128), axis=1)
            for h in range(2):
                s = scores_of(h, start, tokens) + hidden
                before = m_scr[h, :, columns]
                top = jnp.maximum(before, jnp.max(s, axis=0, keepdims=True))
                shrink = jnp.exp2((before - top) * factor)
                weights = jnp.exp2((s - top) * factor)
                m_scr[h, :, columns] = top
                l_scr[h, :, columns] = l_scr[h, :, columns] * shrink + jnp.sum(weights, axis=0, keepdims=True)
                acc[h, :, columns] = acc[h, :, columns] * shrink + weigh(h, weights, tokens)

    for rank in range(cap):
        hide(rank, me, rank)
    attend(stage[0], cap * page)

    @pl.loop(0, full)
    def _(w):
        hide_wave(w * wave, wave)

        @pl.loop(1, n)
        def _(step):
            wave_copy(w, step).wait_recv()

        attend(recv[w], (n - 1) * wave * page)

    @pl.loop(1, n)
    def _(step):
        to, source = partner_pair(me, step, n)
        fresh_copy(step).wait_recv()
        written_ref[source] = fresh_recv[step]

    if rest:
        hide_wave(full * wave, rest)

        @pl.loop(1, n)
        def _(step):
            rest_copy(step).wait_recv()

        attend(rest_recv[...], (n - 1) * rest * page)

    out_block = row_block // 8

    @pl.loop(0, total_rows // row_block)
    def _(index):
        start = pl.multiple_of(index * row_block, row_block)
        columns = pl.ds(start, row_block)
        halves = []
        for h in range(2):
            mixed = acc[h, :, columns] / l_scr[h, :, columns]
            halves.append(mixed.T.reshape(out_block, 8, head_dim))
        out_ref[pl.ds(index * out_block, out_block)] = jnp.concatenate(halves, axis=1).astype(jnp.bfloat16)

    @pl.loop(1, n)
    def _(step):
        @pl.loop(0, full)
        def _(w):
            wave_copy(w, step).wait_send()

        if rest:
            rest_copy(step).wait_send()
        fresh_copy(step).wait_send()


def plan_kernel(
    n, cap, pool_dev, page_size, assign_ref, tokens_ref, table_ref, write_ref,
    plan_ref, ordered, lengths, writes,
):
    me = lax.axis_index("pool")
    max_pages = table_ref.shape[1]
    for d in range(n):
        conversation = assign_ref[d]
        ordered[d:d + 1, :] = table_ref[pl.ds(conversation, 1), :]
        lengths[d:d + 1, :] = jnp.full((1, max_pages), tokens_ref[conversation], jnp.int32)
        writes[d:d + 1, :] = write_ref[pl.ds(conversation, 1), :]
    first = lax.broadcasted_iota(jnp.int32, (n, max_pages), 1) * page_size
    slot = ordered[...] - me * pool_dev
    requested = (slot >= 0) & (slot < pool_dev) & (first < lengths[...])
    row = jnp.broadcast_to(ordered[pl.ds(me, 1), :], (n, max_pages))
    length = jnp.broadcast_to(lengths[pl.ds(me, 1), :], (n, max_pages))
    place = row - lax.broadcasted_iota(jnp.int32, (n, max_pages), 0) * pool_dev
    landed = (place >= 0) & (place < pool_dev) & (first < length)
    values = jnp.concatenate([slot, jnp.minimum(length - first, page_size)], axis=0).astype(jnp.float32)
    marked = jnp.concatenate([jnp.where(requested, 1.0, 0.0), jnp.where(landed, 1.0, 0.0)], axis=0)
    earlier = (
        lax.broadcasted_iota(jnp.int32, (max_pages, max_pages), 0)
        < lax.broadcasted_iota(jnp.int32, (max_pages, max_pages), 1)
    )
    rank = jnp.dot(
        marked.astype(jnp.bfloat16), jnp.where(earlier, 1.0, 0.0).astype(jnp.bfloat16),
        preferred_element_type=jnp.float32,
    )
    rank = jnp.where(marked > 0.0, rank, -1.0)
    lane = lax.broadcasted_iota(jnp.int32, (2 * n, max_pages), 1)
    plan = jnp.zeros((2 * n, max_pages), jnp.float32)
    for r in range(cap):
        column = jnp.sum(jnp.where(rank == r, values, 0.0), axis=1, keepdims=True)
        plan = jnp.where(lane == r, column, plan)
    plan_ref[...] = plan.astype(jnp.int32)
    shape = writes.shape
    own = jnp.broadcast_to(writes[pl.ds(me, 1), :], shape)
    there = own - lax.broadcasted_iota(jnp.int32, shape, 0) * pool_dev
    page = lax.broadcasted_iota(jnp.int32, shape, 1).astype(jnp.float32)
    pick = jnp.sum(jnp.where((there >= 0) & (there < pool_dev), page, 0.0), axis=1, keepdims=True)
    here = writes[...] - me * pool_dev
    target = jnp.min(
        jnp.where((here >= 0) & (here < pool_dev), here, pool_dev).astype(jnp.float32), axis=1, keepdims=True
    )
    lane = lane[0:n, :]
    top = plan[0:n, :]
    top = jnp.where(lane == cap, pick, jnp.where(lane == cap + 1, target, top))
    plan_ref[0:n, :] = top.astype(jnp.int32)


def merge_kernel(
    n, cap, pool_dev, plan_ref, written_ref, attention_ref, pool_ref, out_ref, pool_out_ref,
    tail, held, fresh, out_sem, in_sem,
):
    kept = pool_dev - n
    old = pltpu.make_async_copy(pool_ref.at[pl.ds(0, kept)], pool_out_ref.at[pl.ds(0, kept)], out_sem.at[0])
    result_in = pltpu.make_async_copy(attention_ref, held, in_sem.at[0])
    fresh_in = pltpu.make_async_copy(written_ref, fresh, in_sem.at[1])
    result = pltpu.make_async_copy(held, out_ref, out_sem.at[1])
    last = pltpu.make_async_copy(tail, pool_out_ref.at[pl.ds(kept, n)], out_sem.at[2])
    fresh_in.start()
    result_in.start()
    old.start()
    tail[...] = pool_ref[kept:pool_dev]
    fresh_in.wait()
    for d in range(n):
        @pl.when(plan_ref[d, cap + 1] < pool_dev)
        def _(d=d):
            tail[jnp.maximum(plan_ref[d, cap + 1] - kept, 0)] = fresh[d]
    last.start()
    result_in.wait()
    result.start()
    last.wait()
    result.wait()
    old.wait()


def shards(queries, turn_cache, page_pool, prefix_tokens, prefix_table, write_table, assignment):
    n = lax.axis_size("pool")
    pool_dev, page_size = page_pool.shape[0], page_pool.shape[1]
    head_dim = page_pool.shape[4]
    new_len = queries.shape[0]
    max_pages = prefix_table.shape[1]
    cap = (max_pages + n - 1) // n + 1
    page_rows = page_size * 4
    pages = page_pool.reshape(pool_dev, page_rows, head_dim)
    total_rows = new_len * 8
    row_block = 512
    wave = max(1, 24 // n)
    tokens = max(cap, (n - 1) * wave) * page_size
    smem = pl.BlockSpec(memory_space=pltpu.SMEM)
    vmem = pl.BlockSpec(memory_space=pltpu.VMEM)
    hbm = pl.BlockSpec(memory_space=pltpu.HBM)
    bf16, f32 = jnp.bfloat16, jnp.float32
    plan = pl.pallas_call(
        functools.partial(plan_kernel, n, cap, pool_dev, page_size),
        out_shape=jax.ShapeDtypeStruct((2 * n, max_pages), jnp.int32),
        in_specs=[smem, smem, vmem, vmem],
        out_specs=vmem,
        scratch_shapes=[
            pltpu.VMEM((n, max_pages), jnp.int32),
            pltpu.VMEM((n, max_pages), jnp.int32),
            pltpu.VMEM((n, write_table.shape[1]), jnp.int32),
        ],
    )(assignment, prefix_tokens, prefix_table, write_table)
    attention, written = pl.pallas_call(
        functools.partial(kernel, n, cap, wave, page_rows, row_block),
        out_shape=(
            jax.ShapeDtypeStruct(queries.shape, bf16),
            jax.ShapeDtypeStruct((n, page_rows, head_dim), bf16),
        ),
        in_specs=[smem, hbm, hbm, vmem],
        out_specs=(vmem, vmem),
        scratch_shapes=[
            pltpu.VMEM(queries.shape, bf16),
            pltpu.VMEM((new_len // page_size, page_rows, head_dim), bf16),
            pltpu.SemaphoreType.DMA((2,)),
            pltpu.VMEM((n, cap * page_rows, head_dim), bf16),
            pltpu.VMEM((cap // wave, n - 1, wave * page_rows, head_dim), bf16),
            pltpu.VMEM((n - 1, max(cap % wave, 1) * page_rows, head_dim), bf16),
            pltpu.VMEM((n, page_rows, head_dim), bf16),
            pltpu.VMEM((n, page_rows, head_dim), bf16),
            pltpu.VMEM((2, total_rows, head_dim), bf16),
            pltpu.VMEM((max(tokens, new_len) * 4, head_dim), f32),
            pltpu.VMEM((4, max(tokens, new_len), head_dim), bf16),
            pltpu.VMEM((tokens, 128), f32),
            pltpu.VMEM((2, 1, total_rows), f32),
            pltpu.VMEM((2, 1, total_rows), f32),
            pltpu.VMEM((2, head_dim, total_rows), f32),
            pltpu.SemaphoreType.DMA((cap // wave + 1, n)),
            pltpu.SemaphoreType.DMA((cap // wave + 1, n)),
            pltpu.SemaphoreType.DMA((n,)),
            pltpu.SemaphoreType.DMA((n,)),
        ],
        compiler_params=pltpu.CompilerParams(
            collective_id=0, has_side_effects=True, vmem_limit_bytes=56 * 1024 * 1024
        ),
    )(
        plan, queries,
        turn_cache.reshape(new_len // page_size, page_rows, head_dim),
        pages,
    )
    attention, updated_pool = pl.pallas_call(
        functools.partial(merge_kernel, n, cap, pool_dev),
        out_shape=(
            jax.ShapeDtypeStruct(queries.shape, bf16),
            jax.ShapeDtypeStruct(pages.shape, bf16),
        ),
        in_specs=[smem, hbm, hbm, vmem],
        out_specs=(hbm, hbm),
        scratch_shapes=[
            pltpu.VMEM((n, page_rows, head_dim), bf16),
            pltpu.VMEM(queries.shape, bf16),
            pltpu.VMEM((n, page_rows, head_dim), bf16),
            pltpu.SemaphoreType.DMA((3,)),
            pltpu.SemaphoreType.DMA((2,)),
        ],
        compiler_params=pltpu.CompilerParams(vmem_limit_bytes=56 * 1024 * 1024),
    )(plan, written, attention, pages)
    updated_pool = updated_pool.reshape(page_pool.shape)
    return (attention, updated_pool)


def solution(mesh):
    placed = (
        P(("groups", "pool"), "tensor", None),
        P(("groups", "pool"), None, "tensor", None),
        P(("groups", "pool"), None, None, "tensor", None),
        P("groups"),
        P("groups", None),
        P("groups", None),
        P("groups"),
    )
    return jax.shard_map(
        shards,
        mesh=mesh,
        in_specs=placed,
        out_specs=(
            P(("groups", "pool"), "tensor", None),
            P(("groups", "pool"), None, None, "tensor", None),
        ),
        check_vma=False,
    )
```
